32 devices in a mesh: row: 4 (over x, core), col: 4 (over z), layer: 2 (over y).
Axes of the slice: x: 2, y: 2, z: 4, core: 2. Of those that a mesh axis runs over, the one named last changes fastest.
Arguments:
- interface_panel: float32 [512, 1024], P('col', 'row'), may hold values from -6 to 6
- coupling: float32 [2, 1, 1024, 512], P('layer', None, 'row', 'col'), may hold values from -0.125 to 0.125
- solved_coupling: float32 [2048, 1024], P(('layer', 'col'), 'row'), may hold values from -6 to 6
Outputs:
- schur_panel: float32 [512, 1024], P('col', 'row')
The draws below stay inside these ranges and needn't reach their ends.
All inputs are finite; a program needn't handle non-finite values.
Results may differ from the reference program's by a relative error of at most 0.00007.
Values sent between devices are 32-bit elements; how exact they have to be, the bound alone decides.
No kernel may reach another device: no remote copies, remote signals or barrier semaphores. Data moves between devices by JAX's collectives and lax.ppermute only.
A program may use at most 64 MiB of HBM per device.

```python
import jax
import jax.numpy as jnp
from jax import lax

P_SIZE = 1024
KB = 256
SLOTS = 1
K = 2048
M = 512
N_ROW = 4
N_LAYER = 2


def level_of(stream_key, extent, shards, low, largest):
    def one(axis_at, blocks):
        draws = jax.random.uniform(jax.random.fold_in(jax.random.fold_in(stream_key, 6), axis_at), (blocks,), jnp.float32, low / len(shards), largest / len(shards))
        return jnp.repeat(jnp.exp(draws), extent[axis_at] // blocks).reshape((-1,) + (1,) * (len(extent) - axis_at - 1))

    factor_of = one(*shards[0])
    for cut in shards[1:]:
        factor_of = factor_of * one(*cut)
    return factor_of


def scatter_about(key, shape, scale, bound, pieces=(), kind=jnp.bfloat16):
    level = level_of(key, shape, pieces, -0.22, 0.18) if pieces else 1.0
    result = jax.random.normal(key, shape, jnp.float32) * scale * level
    return jnp.minimum(jnp.maximum(result, -bound), bound).astype(kind)


def setup_inputs(seed: int = 0) -> dict:
    key_of = jax.random.split(jax.random.key(seed), 4)
    interface_panel = scatter_about(key_of[0], (M, P_SIZE), 1.0, 6.0, ((0, 4), (1, 4)), jnp.float32)
    coupling = scatter_about(key_of[1], (N_LAYER, SLOTS, N_ROW * KB, M), K ** -0.5, 0.125, ((0, 2), (2, 4), (3, 4)), jnp.float32)
    solved_coupling = scatter_about(key_of[2], (K, P_SIZE), 1.0, 6.0, ((0, 8), (1, 4)), jnp.float32)
    return {"interface_panel": interface_panel, "coupling": coupling, "solved_coupling": solved_coupling}


def reference(interface_panel, coupling, solved_coupling):
    depth = coupling.shape[0] * coupling.shape[1] * coupling.shape[2]
    coupling_matrix = coupling.reshape(depth, coupling.shape[3])
    product = jnp.dot(coupling_matrix.T, solved_coupling, preferred_element_type=jnp.float32, precision=lax.Precision.HIGHEST)
    return interface_panel - product
```

```python
import jax
import jax.numpy as jnp
from jax import lax
from jax.sharding import PartitionSpec as P

MESH_AXES = ("row", "col", "layer")


def multiply(block, solved):
    return lax.dot_general(
        block,
        solved,
        (((0,), (0,)), ((), ())),
        precision=lax.Precision.HIGH,
        preferred_element_type=jnp.float32,
    )


def from_behind(value, axis, steps):
    count = lax.axis_size(axis)
    pairs = [(source, (source + steps) % count) for source in range(count)]
    return lax.ppermute(value, axis, pairs)


def ring(interface_panel, coupling, solved_coupling):
    blocks = coupling[0]
    rows_here = lax.axis_size("row")
    cols_here = lax.axis_size("col")
    empty = jnp.zeros((blocks.shape[2], solved_coupling.shape[1]), jnp.float32)
    row_id = lax.axis_index("row")
    col_id = lax.axis_index("col")
    for bit in range(cols_here.bit_length() - 1):
        span = 1 << bit
        if span < rows_here:
            moved = from_behind(blocks, "row", -span)
            moved = jnp.where(row_id >= rows_here - span, jnp.roll(moved, -1, axis=0), moved)
        else:
            moved = jnp.roll(blocks, -(span // rows_here), axis=0)
        blocks = jnp.where(col_id // span % 2 == 1, moved, blocks)
    solved = solved_coupling
    for bit in range(rows_here.bit_length() - 1):
        span = 1 << bit
        moved_rows = from_behind(solved, "col", -span)
        solved = jnp.where(row_id // span % 2 == 1, moved_rows, solved)

    def advance(step, carry):
        total, held, current = carry
        total = total + multiply(held[0], current)
        arrived = from_behind(held, "row", -1)
        held = jnp.where(row_id == rows_here - 1, jnp.roll(arrived, -1, axis=0), arrived)
        current = from_behind(current, "col", -1)
        return (total, held, current)

    total, blocks, solved = lax.fori_loop(0, cols_here - 1, advance, (empty, blocks, solved))
    total = total + multiply(blocks[0], solved)
    for step in range(1, lax.axis_size("layer")):
        interface_panel = interface_panel - from_behind(total, "layer", step)
    return interface_panel - total


def is_home(r, c):
    return (r ^ c) & 1 == 0


def route(target):
    pairs = []
    for r in range(4):
        for c in range(4):
            for l in range(2):
                to = target(r, c, l)
                if to is not None:
                    pairs.append((r * 8 + c * 2 + l, to[0] * 8 + to[1] * 2 + to[2]))
    return pairs


def pairs_of_planes(interface_panel, coupling, solved):
    def send(value, target):
        return lax.ppermute(value, MESH_AXES, route(target))

    b = coupling[0, 0]
    r = lax.axis_index("row")
    c = lax.axis_index("col")
    home = is_home(r, c)
    aligned = r // 2 == c // 2
    far = send(solved, lambda r, c, l: (r, c ^ 2, l) if is_home(r, c) else (r ^ 1, c ^ 3, l))
    near = send(solved, lambda r, c, l: None if is_home(r, c) else (r ^ 1, c ^ 1, l))
    b_z = send(b, lambda r, c, l: (r, c ^ 1, l))
    b_x = send(b, lambda r, c, l: (r ^ 2, c, l))
    b_zx = send(b_z, lambda r, c, l: (r ^ 2, c, l))
    far, near, b_z, b_x, b_zx = lax.optimization_barrier((far, near, b_z, b_x, b_zx))
    here = jnp.where(home, solved, near)

    def both(own, other):
        return jnp.concatenate([jnp.where(home, other, own), jnp.where(home, own, other)], 1)

    block_here = both(jnp.where(aligned, b, b_x), jnp.where(aligned, b_z, b_zx))
    block_far = both(jnp.where(aligned, b_x, b), jnp.where(aligned, b_zx, b_z))
    early = multiply(block_here, here)
    early, far = lax.optimization_barrier((early, far))
    total = early + multiply(block_far, far)
    rows = b.shape[1]
    part = total[:rows] + send(total[rows:], lambda r, c, l: (r ^ 1, c, l))
    to_owner = lambda r, c, l: (r, c ^ 1, l) if is_home(r, c) else (r ^ 1, c, l)
    one = send(part, to_owner)
    two = send(part, lambda r, c, l: to_owner(r, c, l)[:2] + (1 - l,))
    return interface_panel - one - two


def solution(mesh):
    small = tuple(mesh.shape[axis] for axis in MESH_AXES) == (4, 4, 2)

    def shards(interface_panel, coupling, solved_coupling):
        if small and coupling.shape[1] == 1 and coupling.shape[2] == solved_coupling.shape[0]:
            return pairs_of_planes(interface_panel, coupling, solved_coupling)
        return ring(interface_panel, coupling, solved_coupling)

    return jax.shard_map(
        shards,
        mesh=mesh,
        in_specs=(P("col", "row"), P("layer", None, "row", "col"), P(("layer", "col"), "row")),
        out_specs=P("col", "row"),
        check_vma=False,
    )
```

```python
import jax
import jax.numpy as jnp
from jax import lax
from jax.sharding import PartitionSpec as P

MESH_AXES = ("row", "col", "layer")


def multiply(block, solved):
    return lax.dot_general(
        block,
        solved,
        (((0,), (0,)), ((), ())),
        precision=lax.Precision.HIGH,
        preferred_element_type=jnp.float32,
    )


def from_behind(value, axis, steps):
    count = lax.axis_size(axis)
    pairs = [(source, (source + steps) % count) for source in range(count)]
    return lax.ppermute(value, axis, pairs)


def ring(interface_panel, coupling, solved_coupling):
    blocks = coupling[0]
    rows_here = lax.axis_size("row")
    cols_here = lax.axis_size("col")
    empty = jnp.zeros((blocks.shape[2], solved_coupling.shape[1]), jnp.float32)
    row_id = lax.axis_index("row")
    col_id = lax.axis_index("col")
    for bit in range(cols_here.bit_length() - 1):
        span = 1 << bit
        if span < rows_here:
            moved = from_behind(blocks, "row", -span)
            moved = jnp.where(row_id >= rows_here - span, jnp.roll(moved, -1, axis=0), moved)
        else:
            moved = jnp.roll(blocks, -(span // rows_here), axis=0)
        blocks = jnp.where(col_id // span % 2 == 1, moved, blocks)
    solved = solved_coupling
    for bit in range(rows_here.bit_length() - 1):
        span = 1 << bit
        moved_rows = from_behind(solved, "col", -span)
        solved = jnp.where(row_id // span % 2 == 1, moved_rows, solved)

    def advance(step, carry):
        total, held, current = carry
        total = total + multiply(held[0], current)
        arrived = from_behind(held, "row", -1)
        held = jnp.where(row_id == rows_here - 1, jnp.roll(arrived, -1, axis=0), arrived)
        current = from_behind(current, "col", -1)
        return (total, held, current)

    total, blocks, solved = lax.fori_loop(0, cols_here - 1, advance, (empty, blocks, solved))
    total = total + multiply(blocks[0], solved)
    for step in range(1, lax.axis_size("layer")):
        interface_panel = interface_panel - from_behind(total, "layer", step)
    return interface_panel - total


def home_parity(c):
    return (c ^ (c >> 1)) & 1


def route(target):
    pairs = []
    for r in range(4):
        for c in range(4):
            for l in range(2):
                r_to, c_to, l_to = target(r, c, l)
                pairs.append((r * 8 + c * 2 + l, r_to * 8 + c_to * 2 + l_to))
    return pairs


def pairs_of_planes(interface_panel, coupling, solved):
    def send(value, target):
        return lax.ppermute(value, MESH_AXES, route(target))

    def fetch(value, source):
        return lax.ppermute(value, MESH_AXES, [(a, b) for b, a in route(source)])

    b = coupling[0, 0]
    r = lax.axis_index("row")
    c = lax.axis_index("col")
    home = r % 2 == home_parity(c)
    aligned = r // 2 == c // 2
    near = fetch(solved, lambda r, c, l: (r & 2 | home_parity(c), c ^ (r ^ c) & 1, l))
    far = fetch(solved, lambda r, c, l: (r & 2 | home_parity(c), c ^ 2 ^ (r ^ c) & 1, l))
    b_z = send(b, lambda r, c, l: (r, c ^ 1, l))
    b_x = send(b, lambda r, c, l: (r ^ 2, c, l))
    b_zx = send(b_z, lambda r, c, l: (r ^ 2, c, l))
    near, far, b_z, b_x, b_zx = lax.optimization_barrier((near, far, b_z, b_x, b_zx))
    y_own = jnp.where(aligned, near, far)
    y_across = jnp.where(aligned, far, near)
    theirs = multiply(jnp.where(home, b, b_z), y_own) + multiply(jnp.where(home, b_x, b_zx), y_across)
    theirs = send(theirs, lambda r, c, l: (r ^ 1, c, l))
    mine = multiply(jnp.where(home, b_z, b), y_own) + multiply(jnp.where(home, b_zx, b_x), y_across)
    part = mine + theirs

    def to_owner(r, c, l):
        return (r, c ^ 1, l) if r % 2 == home_parity(c) else (r ^ 1, c, l)

    other_layer = send(part, lambda r, c, l: to_owner(r, c, 1 - l))
    this_layer = send(part, to_owner)
    return interface_panel - other_layer - this_layer


def solution(mesh):
    small = tuple(mesh.shape[axis] for axis in MESH_AXES) == (4, 4, 2)

    def shards(interface_panel, coupling, solved_coupling):
        if small and coupling.shape[1] == 1 and coupling.shape[2] == solved_coupling.shape[0]:
            return pairs_of_planes(interface_panel, coupling, solved_coupling)
        return ring(interface_panel, coupling, solved_coupling)

    return jax.shard_map(
        shards,
        mesh=mesh,
        in_specs=(P("col", "row"), P("layer", None, "row", "col"), P(("layer", "col"), "row")),
        out_specs=P("col", "row"),
        check_vma=False,
    )
```

```python
import jax
import jax.numpy as jnp
from jax import lax
from jax.sharding import PartitionSpec as P

MESH_AXES = ("row", "col", "layer")


def multiply(block, solved):
    return lax.dot_general(
        block,
        solved,
        (((0,), (0,)), ((), ())),
        precision=lax.Precision.HIGH,
        preferred_element_type=jnp.float32,
    )


def from_behind(value, axis, steps):
    count = lax.axis_size(axis)
    pairs = [(source, (source + steps) % count) for source in range(count)]
    return lax.ppermute(value, axis, pairs)


def ring(interface_panel, coupling, solved_coupling):
    blocks = coupling[0]
    rows_here = lax.axis_size("row")
    cols_here = lax.axis_size("col")
    empty = jnp.zeros((blocks.shape[2], solved_coupling.shape[1]), jnp.float32)
    row_id = lax.axis_index("row")
    col_id = lax.axis_index("col")
    for bit in range(cols_here.bit_length() - 1):
        span = 1 << bit
        if span < rows_here:
            moved = from_behind(blocks, "row", -span)
            moved = jnp.where(row_id >= rows_here - span, jnp.roll(moved, -1, axis=0), moved)
        else:
            moved = jnp.roll(blocks, -(span // rows_here), axis=0)
        blocks = jnp.where(col_id // span % 2 == 1, moved, blocks)
    solved = solved_coupling
    for bit in range(rows_here.bit_length() - 1):
        span = 1 << bit
        moved_rows = from_behind(solved, "col", -span)
        solved = jnp.where(row_id // span % 2 == 1, moved_rows, solved)

    def advance(step, carry):
        total, held, current = carry
        total = total + multiply(held[0], current)
        arrived = from_behind(held, "row", -1)
        held = jnp.where(row_id == rows_here - 1, jnp.roll(arrived, -1, axis=0), arrived)
        current = from_behind(current, "col", -1)
        return (total, held, current)

    total, blocks, solved = lax.fori_loop(0, cols_here - 1, advance, (empty, blocks, solved))
    total = total + multiply(blocks[0], solved)
    for step in range(1, lax.axis_size("layer")):
        interface_panel = interface_panel - from_behind(total, "layer", step)
    return interface_panel - total


def is_home(r, c):
    return (r ^ c) & 1 == 0


def route(target):
    pairs = []
    for r in range(4):
        for c in range(4):
            for l in range(2):
                r_to, c_to, l_to = target(r, c, l)
                pairs.append((r * 8 + c * 2 + l, r_to * 8 + c_to * 2 + l_to))
    return pairs


def pairs_of_planes(interface_panel, coupling, solved):
    def send(value, target):
        return lax.ppermute(value, MESH_AXES, route(target))

    b = coupling[0, 0]
    r = lax.axis_index("row")
    c = lax.axis_index("col")
    home = is_home(r, c)
    aligned = r // 2 == c // 2
    near = send(solved, lambda r, c, l: (r, c, l) if is_home(r, c) else (r ^ 1, c ^ 1, l))
    far = send(solved, lambda r, c, l: (r, c ^ 2, l) if is_home(r, c) else (r ^ 1, c ^ 3, l))
    b_z = send(b, lambda r, c, l: (r, c ^ 1, l))
    b_x = send(b, lambda r, c, l: (r ^ 2, c, l))
    b_zx = send(b_z, lambda r, c, l: (r ^ 2, c, l))
    near, far, b_z, b_x, b_zx = lax.optimization_barrier((near, far, b_z, b_x, b_zx))
    y_own = jnp.where(aligned, near, far)
    y_across = jnp.where(aligned, far, near)
    theirs = multiply(jnp.where(home, b, b_z), y_own) + multiply(jnp.where(home, b_x, b_zx), y_across)
    theirs, b_x, b_zx = lax.optimization_barrier((theirs, b_x, b_zx))
    theirs = send(theirs, lambda r, c, l: (r ^ 1, c, l))
    mine = multiply(jnp.where(home, b_z, b), y_own) + multiply(jnp.where(home, b_zx, b_x), y_across)
    part = lax.optimization_barrier(mine) + theirs

    def to_owner(r, c, l):
        return (r, c ^ 1, l) if is_home(r, c) else (r ^ 1, c, l)

    this_layer = send(part, to_owner)
    other_layer = send(part, lambda r, c, l: to_owner(r, c, 1 - l))
    return interface_panel - this_layer - other_layer


def solution(mesh):
    small = tuple(mesh.shape[axis] for axis in MESH_AXES) == (4, 4, 2)

    def shards(interface_panel, coupling, solved_coupling):
        if small and coupling.shape[1] == 1 and coupling.shape[2] == solved_coupling.shape[0]:
            return pairs_of_planes(interface_panel, coupling, solved_coupling)
        return ring(interface_panel, coupling, solved_coupling)

    return jax.shard_map(
        shards,
        mesh=mesh,
        in_specs=(P("col", "row"), P("layer", None, "row", "col"), P(("layer", "col"), "row")),
        out_specs=P("col", "row"),
        check_vma=False,
    )
```

```python
import jax
import jax.numpy as jnp
from jax import lax
from jax.sharding import PartitionSpec as P

MESH_AXES = ("row", "col", "layer")


def multiply(block, solved):
    return lax.dot_general(
        block,
        solved,
        (((0,), (0,)), ((), ())),
        precision=lax.Precision.HIGH,
        preferred_element_type=jnp.float32,
    )


def from_behind(value, axis, steps):
    count = lax.axis_size(axis)
    pairs = [(source, (source + steps) % count) for source in range(count)]
    return lax.ppermute(value, axis, pairs)


def ring(interface_panel, coupling, solved_coupling):
    blocks = coupling[0]
    rows_here = lax.axis_size("row")
    cols_here = lax.axis_size("col")
    empty = jnp.zeros((blocks.shape[2], solved_coupling.shape[1]), jnp.float32)
    row_id = lax.axis_index("row")
    col_id = lax.axis_index("col")
    for bit in range(cols_here.bit_length() - 1):
        span = 1 << bit
        if span < rows_here:
            moved = from_behind(blocks, "row", -span)
            moved = jnp.where(row_id >= rows_here - span, jnp.roll(moved, -1, axis=0), moved)
        else:
            moved = jnp.roll(blocks, -(span // rows_here), axis=0)
        blocks = jnp.where(col_id // span % 2 == 1, moved, blocks)
    solved = solved_coupling
    for bit in range(rows_here.bit_length() - 1):
        span = 1 << bit
        moved_rows = from_behind(solved, "col", -span)
        solved = jnp.where(row_id // span % 2 == 1, moved_rows, solved)

    def advance(step, carry):
        total, held, current = carry
        total = total + multiply(held[0], current)
        arrived = from_behind(held, "row", -1)
        held = jnp.where(row_id == rows_here - 1, jnp.roll(arrived, -1, axis=0), arrived)
        current = from_behind(current, "col", -1)
        return (total, held, current)

    total, blocks, solved = lax.fori_loop(0, cols_here - 1, advance, (empty, blocks, solved))
    total = total + multiply(blocks[0], solved)
    for step in range(1, lax.axis_size("layer")):
        interface_panel = interface_panel - from_behind(total, "layer", step)
    return interface_panel - total


def is_home(r, c):
    return (r ^ c) & 1 == 0


def route(target):
    pairs = []
    for r in range(4):
        for c in range(4):
            for l in range(2):
                r_to, c_to, l_to = target(r, c, l)
                pairs.append((r * 8 + c * 2 + l, r_to * 8 + c_to * 2 + l_to))
    return pairs


def pairs_of_planes(interface_panel, coupling, solved):
    def send(value, target):
        return lax.ppermute(value, MESH_AXES, route(target))

    b = coupling[0, 0]
    r = lax.axis_index("row")
    c = lax.axis_index("col")
    home = is_home(r, c)
    aligned = r // 2 == c // 2
    other = send(solved, lambda r, c, l: (r ^ 1, c, l))
    near = send(other, lambda r, c, l: (r, c ^ 1, l) if is_home(r, c) else (r ^ 1, c, l))
    far = send(other, lambda r, c, l: (r, c ^ 3, l) if is_home(r, c) else (r ^ 1, c ^ 2, l))
    b_z = send(b, lambda r, c, l: (r, c ^ 1, l))
    b_x = send(b, lambda r, c, l: (r ^ 2, c, l))
    b_zx = send(b_z, lambda r, c, l: (r ^ 2, c, l))
    near, far, b_z, b_x, b_zx = lax.optimization_barrier((near, far, b_z, b_x, b_zx))
    y_own = jnp.where(aligned, near, far)
    y_across = jnp.where(aligned, far, near)
    theirs = multiply(
        jnp.concatenate([jnp.where(home, b, b_z), jnp.where(home, b_x, b_zx)]),
        jnp.concatenate([y_own, y_across]),
    )
    theirs, b_x, b_zx = lax.optimization_barrier((theirs, b_x, b_zx))
    theirs = send(theirs, lambda r, c, l: (r ^ 1, c, l))
    mine = multiply(jnp.where(home, b_z, b), y_own) + multiply(jnp.where(home, b_zx, b_x), y_across)
    part = lax.optimization_barrier(mine) + theirs
    one = send(part, lambda r, c, l: (r, c ^ 1, 1 - l) if is_home(r, c) else (r ^ 1, c, l))
    two = send(part, lambda r, c, l: (r, c ^ 1, l) if is_home(r, c) else (r ^ 1, c, 1 - l))
    return interface_panel - one - two


def solution(mesh):
    small = tuple(mesh.shape[axis] for axis in MESH_AXES) == (4, 4, 2)

    def shards(interface_panel, coupling, solved_coupling):
        if small and coupling.shape[1] == 1 and coupling.shape[2] == solved_coupling.shape[0]:
            return pairs_of_planes(interface_panel, coupling, solved_coupling)
        return ring(interface_panel, coupling, solved_coupling)

    return jax.shard_map(
        shards,
        mesh=mesh,
        in_specs=(P("col", "row"), P("layer", None, "row", "col"), P(("layer", "col"), "row")),
        out_specs=P("col", "row"),
        check_vma=False,
    )
```

```python
import jax
import jax.numpy as jnp
from jax import lax
from jax.sharding import PartitionSpec as P

MESH_AXES = ("row", "col", "layer")


def multiply(block, solved):
    return lax.dot_general(
        block,
        solved,
        (((0,), (0,)), ((), ())),
        precision=lax.Precision.HIGH,
        preferred_element_type=jnp.float32,
    )


def from_behind(value, axis, steps):
    count = lax.axis_size(axis)
    pairs = [(source, (source + steps) % count) for source in range(count)]
    return lax.ppermute(value, axis, pairs)


def ring(interface_panel, coupling, solved_coupling):
    blocks = coupling[0]
    rows_here = lax.axis_size("row")
    cols_here = lax.axis_size("col")
    empty = jnp.zeros((blocks.shape[2], solved_coupling.shape[1]), jnp.float32)
    row_id = lax.axis_index("row")
    col_id = lax.axis_index("col")
    for bit in range(cols_here.bit_length() - 1):
        span = 1 << bit
        if span < rows_here:
            moved = from_behind(blocks, "row", -span)
            moved = jnp.where(row_id >= rows_here - span, jnp.roll(moved, -1, axis=0), moved)
        else:
            moved = jnp.roll(blocks, -(span // rows_here), axis=0)
        blocks = jnp.where(col_id // span % 2 == 1, moved, blocks)
    solved = solved_coupling
    for bit in range(rows_here.bit_length() - 1):
        span = 1 << bit
        moved_rows = from_behind(solved, "col", -span)
        solved = jnp.where(row_id // span % 2 == 1, moved_rows, solved)

    def advance(step, carry):
        total, held, current = carry
        total = total + multiply(held[0], current)
        arrived = from_behind(held, "row", -1)
        held = jnp.where(row_id == rows_here - 1, jnp.roll(arrived, -1, axis=0), arrived)
        current = from_behind(current, "col", -1)
        return (total, held, current)

    total, blocks, solved = lax.fori_loop(0, cols_here - 1, advance, (empty, blocks, solved))
    total = total + multiply(blocks[0], solved)
    for step in range(1, lax.axis_size("layer")):
        interface_panel = interface_panel - from_behind(total, "layer", step)
    return interface_panel - total


def is_home(r, c):
    return (r ^ c) & 1 == 0


def route(target):
    pairs = []
    for r in range(4):
        for c in range(4):
            for l in range(2):
                r_to, c_to, l_to = target(r, c, l)
                pairs.append((r * 8 + c * 2 + l, r_to * 8 + c_to * 2 + l_to))
    return pairs


def pairs_of_planes(interface_panel, coupling, solved):
    def send(value, target):
        return lax.ppermute(value, MESH_AXES, route(target))

    b = coupling[0, 0]
    r = lax.axis_index("row")
    c = lax.axis_index("col")
    home = is_home(r, c)
    aligned = r // 2 == c // 2
    other = send(solved, lambda r, c, l: (r ^ 1, c, l))
    far = send(other, lambda r, c, l: (r, c ^ 3, l) if is_home(r, c) else (r ^ 1, c ^ 2, l))
    near = send(other, lambda r, c, l: (r, c ^ 1, l) if is_home(r, c) else (r ^ 1, c, l))
    b_z = send(b, lambda r, c, l: (r, c ^ 1, l))
    b_x = send(b, lambda r, c, l: (r ^ 2, c, l))
    b_zx = send(b_z, lambda r, c, l: (r ^ 2, c, l))
    near, far, b_z, b_x, b_zx = lax.optimization_barrier((near, far, b_z, b_x, b_zx))
    y = jnp.concatenate([jnp.where(aligned, near, far), jnp.where(aligned, far, near)])
    theirs = multiply(jnp.concatenate([jnp.where(home, b, b_z), jnp.where(home, b_x, b_zx)]), y)
    theirs, b_x, b_zx = lax.optimization_barrier((theirs, b_x, b_zx))
    theirs = send(theirs, lambda r, c, l: (r ^ 1, c, l))
    mine = multiply(jnp.concatenate([jnp.where(home, b_z, b), jnp.where(home, b_zx, b_x)]), y)
    part = lax.optimization_barrier(mine) + theirs
    one = send(part, lambda r, c, l: (r, c ^ 1, 1 - l) if is_home(r, c) else (r ^ 1, c, l))
    two = send(part, lambda r, c, l: (r, c ^ 1, l) if is_home(r, c) else (r ^ 1, c, 1 - l))
    return interface_panel - one - two


def solution(mesh):
    small = tuple(mesh.shape[axis] for axis in MESH_AXES) == (4, 4, 2)

    def shards(interface_panel, coupling, solved_coupling):
        if small and coupling.shape[1] == 1 and coupling.shape[2] == solved_coupling.shape[0]:
            return pairs_of_planes(interface_panel, coupling, solved_coupling)
        return ring(interface_panel, coupling, solved_coupling)

    return jax.shard_map(
        shards,
        mesh=mesh,
        in_specs=(P("col", "row"), P("layer", None, "row", "col"), P(("layer", "col"), "row")),
        out_specs=P("col", "row"),
        check_vma=False,
    )
```

```python
import jax
import jax.numpy as jnp
from jax import lax
from jax.sharding import PartitionSpec as P

MESH_AXES = ("row", "col", "layer")


def multiply(block, solved):
    return lax.dot_general(
        block,
        solved,
        (((0,), (0,)), ((), ())),
        precision=lax.Precision.HIGH,
        preferred_element_type=jnp.float32,
    )


def from_behind(value, axis, steps):
    count = lax.axis_size(axis)
    pairs = [(source, (source + steps) % count) for source in range(count)]
    return lax.ppermute(value, axis, pairs)


def ring(interface_panel, coupling, solved_coupling):
    blocks = coupling[0]
    rows_here = lax.axis_size("row")
    cols_here = lax.axis_size("col")
    empty = jnp.zeros((blocks.shape[2], solved_coupling.shape[1]), jnp.float32)
    row_id = lax.axis_index("row")
    col_id = lax.axis_index("col")
    for bit in range(cols_here.bit_length() - 1):
        span = 1 << bit
        if span < rows_here:
            moved = from_behind(blocks, "row", -span)
            moved = jnp.where(row_id >= rows_here - span, jnp.roll(moved, -1, axis=0), moved)
        else:
            moved = jnp.roll(blocks, -(span // rows_here), axis=0)
        blocks = jnp.where(col_id // span % 2 == 1, moved, blocks)
    solved = solved_coupling
    for bit in range(rows_here.bit_length() - 1):
        span = 1 << bit
        moved_rows = from_behind(solved, "col", -span)
        solved = jnp.where(row_id // span % 2 == 1, moved_rows, solved)

    def advance(step, carry):
        total, held, current = carry
        total = total + multiply(held[0], current)
        arrived = from_behind(held, "row", -1)
        held = jnp.where(row_id == rows_here - 1, jnp.roll(arrived, -1, axis=0), arrived)
        current = from_behind(current, "col", -1)
        return (total, held, current)

    total, blocks, solved = lax.fori_loop(0, cols_here - 1, advance, (empty, blocks, solved))
    total = total + multiply(blocks[0], solved)
    for step in range(1, lax.axis_size("layer")):
        interface_panel = interface_panel - from_behind(total, "layer", step)
    return interface_panel - total


def is_home(r, c):
    return (r ^ c) & 1 == 0


def route(target):
    pairs = []
    for r in range(4):
        for c in range(4):
            for l in range(2):
                r_to, c_to, l_to = target(r, c, l)
                pairs.append((r * 8 + c * 2 + l, r_to * 8 + c_to * 2 + l_to))
    return pairs


def pairs_of_planes(interface_panel, coupling, solved):
    def send(value, target):
        return lax.ppermute(value, MESH_AXES, route(target))

    b = coupling[0, 0]
    r = lax.axis_index("row")
    c = lax.axis_index("col")
    home = is_home(r, c)
    aligned = r // 2 == c // 2
    other = send(solved, lambda r, c, l: (r ^ 1, c, l))
    far = send(other, lambda r, c, l: (r, c ^ 3, l) if is_home(r, c) else (r ^ 1, c ^ 2, l))
    near = send(other, lambda r, c, l: (r, c ^ 1, l) if is_home(r, c) else (r ^ 1, c, l))
    b_z = send(b, lambda r, c, l: (r, c ^ 1, l))
    b_x = send(b, lambda r, c, l: (r ^ 2, c, l))
    b_zx = send(b_z, lambda r, c, l: (r ^ 2, c, l))
    far, near, b_z, b_x, b_zx = lax.optimization_barrier((far, near, b_z, b_x, b_zx))
    y = jnp.concatenate([jnp.where(aligned, near, far), jnp.where(aligned, far, near)])
    theirs = multiply(jnp.concatenate([jnp.where(home, b, b_z), jnp.where(home, b_x, b_zx)]), y)
    theirs, b_x, b_zx = lax.optimization_barrier((theirs, b_x, b_zx))
    theirs = send(theirs, lambda r, c, l: (r ^ 1, c, l))
    mine = multiply(jnp.concatenate([jnp.where(home, b_z, b), jnp.where(home, b_zx, b_x)]), y)
    part = lax.optimization_barrier(mine) + theirs
    one = send(part, lambda r, c, l: (r, c ^ 1, 1 - l) if is_home(r, c) else (r ^ 1, c, l))
    two = send(part, lambda r, c, l: (r, c ^ 1, l) if is_home(r, c) else (r ^ 1, c, 1 - l))
    return interface_panel - one - two


def solution(mesh):
    small = tuple(mesh.shape[axis] for axis in MESH_AXES) == (4, 4, 2)

    def shards(interface_panel, coupling, solved_coupling):
        if small and coupling.shape[1] == 1 and coupling.shape[2] == solved_coupling.shape[0]:
            return pairs_of_planes(interface_panel, coupling, solved_coupling)
        return ring(interface_panel, coupling, solved_coupling)

    return jax.shard_map(
        shards,
        mesh=mesh,
        in_specs=(P("col", "row"), P("layer", None, "row", "col"), P(("layer", "col"), "row")),
        out_specs=P("col", "row"),
        check_vma=False,
    )
```

```python
import jax
import jax.numpy as jnp
from jax import lax
from jax.sharding import PartitionSpec as P

MESH_AXES = ("row", "col", "layer")


def multiply(block, solved):
    return lax.dot_general(
        block,
        solved,
        (((0,), (0,)), ((), ())),
        precision=lax.Precision.HIGH,
        preferred_element_type=jnp.float32,
    )


def from_behind(value, axis, steps):
    count = lax.axis_size(axis)
    pairs = [(source, (source + steps) % count) for source in range(count)]
    return lax.ppermute(value, axis, pairs)


def ring(interface_panel, coupling, solved_coupling):
    blocks = coupling[0]
    rows_here = lax.axis_size("row")
    cols_here = lax.axis_size("col")
    empty = jnp.zeros((blocks.shape[2], solved_coupling.shape[1]), jnp.float32)
    row_id = lax.axis_index("row")
    col_id = lax.axis_index("col")
    for bit in range(cols_here.bit_length() - 1):
        span = 1 << bit
        if span < rows_here:
            moved = from_behind(blocks, "row", -span)
            moved = jnp.where(row_id >= rows_here - span, jnp.roll(moved, -1, axis=0), moved)
        else:
            moved = jnp.roll(blocks, -(span // rows_here), axis=0)
        blocks = jnp.where(col_id // span % 2 == 1, moved, blocks)
    solved = solved_coupling
    for bit in range(rows_here.bit_length() - 1):
        span = 1 << bit
        moved_rows = from_behind(solved, "col", -span)
        solved = jnp.where(row_id // span % 2 == 1, moved_rows, solved)

    def advance(step, carry):
        total, held, current = carry
        total = total + multiply(held[0], current)
        arrived = from_behind(held, "row", -1)
        held = jnp.where(row_id == rows_here - 1, jnp.roll(arrived, -1, axis=0), arrived)
        current = from_behind(current, "col", -1)
        return (total, held, current)

    total, blocks, solved = lax.fori_loop(0, cols_here - 1, advance, (empty, blocks, solved))
    total = total + multiply(blocks[0], solved)
    for step in range(1, lax.axis_size("layer")):
        interface_panel = interface_panel - from_behind(total, "layer", step)
    return interface_panel - total


def is_home(r, c):
    return (r ^ c) & 1 == 0


def route(target):
    pairs = []
    for r in range(4):
        for c in range(4):
            for l in range(2):
                r_to, c_to, l_to = target(r, c, l)
                pairs.append((r * 8 + c * 2 + l, r_to * 8 + c_to * 2 + l_to))
    return pairs


def pairs_of_planes(interface_panel, coupling, solved):
    def send(value, target):
        return lax.ppermute(value, MESH_AXES, route(target))

    b = coupling[0, 0]
    r = lax.axis_index("row")
    c = lax.axis_index("col")
    home = is_home(r, c)
    aligned = r // 2 == c // 2
    other = send(solved, lambda r, c, l: (r ^ 1, c, l))
    far = send(other, lambda r, c, l: (r, c ^ 3, l) if is_home(r, c) else (r ^ 1, c ^ 2, l))
    near = send(other, lambda r, c, l: (r, c ^ 1, l) if is_home(r, c) else (r ^ 1, c, l))
    b_z = send(b, lambda r, c, l: (r, c ^ 1, l))
    b_x = send(b, lambda r, c, l: (r ^ 2, c, l))
    b_zx = send(b_z, lambda r, c, l: (r ^ 2, c, l))
    far, near, b_z, b_x, b_zx = lax.optimization_barrier((far, near, b_z, b_x, b_zx))
    y = jnp.concatenate([jnp.where(aligned, near, far), jnp.where(aligned, far, near)])
    theirs = multiply(jnp.concatenate([jnp.where(home, b, b_z), jnp.where(home, b_x, b_zx)]), y)
    theirs, b_x, b_zx = lax.optimization_barrier((theirs, b_x, b_zx))
    theirs = send(theirs, lambda r, c, l: (r ^ 1, c, l))
    mine = multiply(jnp.concatenate([jnp.where(home, b_z, b), jnp.where(home, b_zx, b_x)]), y)
    part = lax.optimization_barrier(mine) + theirs
    one = send(part, lambda r, c, l: (r, c ^ 1, 1 - l) if is_home(r, c) else (r ^ 1, c, l))
    two = send(part, lambda r, c, l: (r, c ^ 1, l) if is_home(r, c) else (r ^ 1, c, 1 - l))
    return interface_panel - two - one


def solution(mesh):
    small = tuple(mesh.shape[axis] for axis in MESH_AXES) == (4, 4, 2)

    def shards(interface_panel, coupling, solved_coupling):
        if small and coupling.shape[1] == 1 and coupling.shape[2] == solved_coupling.shape[0]:
            return pairs_of_planes(interface_panel, coupling, solved_coupling)
        return ring(interface_panel, coupling, solved_coupling)

    return jax.shard_map(
        shards,
        mesh=mesh,
        in_specs=(P("col", "row"), P("layer", None, "row", "col"), P(("layer", "col"), "row")),
        out_specs=P("col", "row"),
        check_vma=False,
    )
```
